32 devices in a mesh: req: 8 (over z, x), tp: 4 (over y, core).
Axes of the slice: x: 2, y: 2, z: 4, core: 2. Of those that a mesh axis runs over, the one named last changes fastest.
Arguments:
- tokens: bfloat16 [4096, 2048], P('req', 'tp'), may hold values from -6 to 6
- first_gain: float32 [2048], replicated, may hold values from 0.5 to 1.5
- first_shift: float32 [2048], replicated, may hold values from -2.5 to 2.5
- project_weight: bfloat16 [2048, 3, 2048], P(None, None, 'tp'), may hold values from -0.125 to 0.125
- project_bias: float32 [3, 2048], P(None, 'tp'), may hold values from -3 to 3
- output_weight: bfloat16 [2048, 2048], P('tp'), may hold values from -0.125 to 0.125
- second_gain: float32 [2048], replicated, may hold values from 0.5 to 1.5
- second_shift: float32 [2048], replicated, may hold values from -2.5 to 2.5
- expand_weight: bfloat16 [2048, 2, 3072], P(None, None, 'tp'), may hold values from -0.125 to 0.125
- contract_weight: bfloat16 [3072, 2048], P('tp'), may hold values from -0.109375 to 0.109375
- prior_cache: bfloat16 [8, 1024, 2, 2048], P('req', None, None, 'tp'), may hold values from -21 to 21
- prior_len: int32 [8], replicated, may hold values from 16 to 1024, as said below
- slot_map: int32 [8], replicated, may hold values from 0 to 7, each once
- block_table: int32 [8, 6], replicated, may hold values from 0 to 11, as said below
Outputs:
- mixed_out: bfloat16 [4096, 2048], P('req', 'tp')
- page_pool: bfloat16 [8, 12, 256, 2, 1024], P('req', None, None, None, 'tp')
The draws below stay inside these ranges and needn't reach their ends.
Inputs may be any that keep to these rules, and one draw needn't show every extreme that they name: `prior_len`: every request has at least 16 cached positions; some request has exactly 1024. `block_table`: rows 2g and 2g+1 together name each of the 12 pages exactly once.
All inputs are finite; a program needn't handle non-finite values.
Results may differ from the reference program's by a relative error of at most 0.018.
Values may be sent and summed in bfloat16 or wider, within the bound.
A program may use at most 128 MiB of HBM per device.

```python
import jax
import jax.numpy as jnp
from jax import lax

D = 2048
HEADS = 32
HEAD_DIM = 64
ROTARY = 16
FF = 3072
STRETCH = 512
BLOCK = 256
MAX_PRIOR = 1024
REQUESTS = 8
TOKENS = 4096
BLOCKS = 6
PAGES = 12
N_TP = 4


def draw_project_bias(key, part):
    base_draw = jnp.clip(0.5 * jax.random.normal(jax.random.fold_in(key, 11), (3, HEADS, HEAD_DIM), jnp.float32), -2.5, 2.5)
    return base_draw.reshape(3, HEADS * HEAD_DIM)


def draw_prior_cache(key, part):
    normal_draw = jnp.clip(jax.random.normal(jax.random.fold_in(key, 12), (REQUESTS, MAX_PRIOR, 2, HEADS, HEAD_DIM), jnp.float32), -6.0, 6.0)
    return normal_draw.reshape(REQUESTS, MAX_PRIOR, 2, HEADS * HEAD_DIM).astype(jnp.bfloat16)


def draw_prior_len(key, part):
    lengths = jax.random.randint(jax.random.fold_in(key, 14), (REQUESTS,), 16, MAX_PRIOR + 1, jnp.int32)
    longest = jax.random.randint(jax.random.fold_in(key, 15), (), 0, REQUESTS, jnp.int32)
    return lengths.at[longest].set(MAX_PRIOR)


def draw_block_table(key, part):
    group_keys = jax.random.split(jax.random.fold_in(key, 16), REQUESTS // 2)
    page_perms = jax.vmap(lambda group_key: jax.random.permutation(group_key, PAGES))(group_keys)
    return page_perms.reshape(REQUESTS, BLOCKS).astype(jnp.int32)


def levels(key, shape, shards, low, top_value):
    factor_of, own = 1.0, jax.random.fold_in(key, 6)
    for axis_at, shards_of in shards:
        heights = jnp.exp(jax.random.uniform(jax.random.fold_in(own, axis_at), (shards_of,), jnp.float32, low / len(shards), top_value / len(shards)))
        factor_of = factor_of * jnp.repeat(heights, shape[axis_at] // shards_of).reshape([-1 if axis == axis_at else 1 for axis in range(len(shape))])
    return factor_of


def bell_draw(own_key, shape, deviation, limit, pieces=(), kind=jnp.bfloat16):
    drawn = deviation * jax.random.normal(own_key, shape, jnp.float32)
    if pieces:
        drawn = drawn * levels(own_key, shape, pieces, -0.22, 0.18)
    return jnp.clip(drawn, -limit, limit).astype(kind)


def setup_inputs(seed: int = 0) -> dict:
    arg_keys = jax.random.split(jax.random.key(seed), 15)
    tokens = bell_draw(arg_keys[0], (TOKENS, D), 1.0, 6.0, ((0, 8), (1, 4)))
    first_gain = jnp.clip(1.0 + 0.1 * jax.random.normal(arg_keys[1], (D,), jnp.float32), 0.5, 1.5)
    first_shift = bell_draw(arg_keys[2], (D,), 0.3, 2.5, (), jnp.float32)
    project_weight = bell_draw(arg_keys[3], (D, 3, HEADS * HEAD_DIM), D ** -0.5, 0.125, ((2, 4),))
    project_bias = draw_project_bias(jax.random.fold_in(arg_keys[14], 71), 0)
    output_weight = bell_draw(arg_keys[5], (HEADS * HEAD_DIM, D), (HEADS * HEAD_DIM) ** -0.5, 0.125, ((0, 4),))
    second_gain = jnp.clip(1.0 + 0.1 * jax.random.normal(arg_keys[6], (D,), jnp.float32), 0.5, 1.5)
    second_shift = bell_draw(arg_keys[7], (D,), 0.3, 2.5, (), jnp.float32)
    expand_weight = bell_draw(arg_keys[8], (D, 2, FF), D ** -0.5, 0.125, ((2, 4),))
    contract_weight = bell_draw(arg_keys[9], (FF, D), FF ** -0.5, 0.109375, ((0, 4),))
    prior_cache = draw_prior_cache(jax.random.fold_in(arg_keys[14], 71), 0)
    prior_len = draw_prior_len(jax.random.fold_in(arg_keys[14], 71), 0)
    slot_map = jax.random.permutation(arg_keys[12], REQUESTS).astype(jnp.int32)
    block_table = draw_block_table(jax.random.fold_in(arg_keys[14], 71), 0)
    return {"tokens": tokens, "first_gain": first_gain, "first_shift": first_shift, "project_weight": project_weight, "project_bias": project_bias, "output_weight": output_weight, "second_gain": second_gain, "second_shift": second_shift, "expand_weight": expand_weight, "contract_weight": contract_weight, "prior_cache": prior_cache, "prior_len": prior_len, "slot_map": slot_map, "block_table": block_table}


EPSILON = 1e-05
ROPE_BASE = 10000.0
MASK_FILL = -1e+30

def layer_norm(inputs, gain_row, shift_row):
    center = inputs - lax.optimization_barrier(jnp.mean(inputs, axis=-1, keepdims=True))
    spread = lax.optimization_barrier(jnp.mean(center * center, axis=-1, keepdims=True))
    return (center * lax.rsqrt(spread + EPSILON) * gain_row + shift_row).astype(jnp.bfloat16)

def rotate(values, positions):
    half_rot = ROTARY // 2
    frequency = ROPE_BASE ** (-2.0 * jnp.arange(half_rot, dtype=jnp.float32) / ROTARY)
    angles = positions.astype(jnp.float32)[:, None] * frequency[None, :]
    cosine = jnp.cos(angles)[:, None, :]
    sine_part = jnp.sin(angles)[:, None, :]
    first_half = values[..., :half_rot]
    second_half = values[..., half_rot:ROTARY]
    return jnp.concatenate([first_half * cosine - second_half * sine_part, second_half * cosine + first_half * sine_part, values[..., ROTARY:]], axis=-1)

def attend(queries, key_rows, value_rows, prior_count):
    query_count = queries.shape[0]
    cache_rows = key_rows.shape[0] - query_count
    scores = jnp.einsum('qhd,khd->hqk', queries.astype(jnp.float32), key_rows.astype(jnp.float32)) * HEAD_DIM ** (-0.5)
    key_index = jnp.arange(key_rows.shape[0], dtype=jnp.int32)[None, :]
    query_index = jnp.arange(query_count, dtype=jnp.int32)[:, None]
    allowed = jnp.where(key_index < cache_rows, key_index < prior_count, key_index - cache_rows <= query_index)
    scores = jnp.where(allowed[None], scores, MASK_FILL)
    highest = lax.optimization_barrier(jnp.max(scores, axis=-1, keepdims=True))
    weights = jnp.exp(scores - highest)
    normalized = (weights / lax.optimization_barrier(jnp.sum(weights, axis=-1, keepdims=True))).astype(jnp.bfloat16)
    mixture = jnp.einsum('hqk,khd->qhd', normalized.astype(jnp.float32), value_rows.astype(jnp.float32))
    return mixture.astype(jnp.bfloat16)

def summed_parts(left_rows, right_rows):
    block_width = left_rows.shape[1] // N_TP
    summed = jnp.zeros((left_rows.shape[0], right_rows.shape[1]), jnp.float32)
    for part_index in range(N_TP):
        partial_term = jnp.dot(left_rows[:, part_index * block_width:(part_index + 1) * block_width], right_rows[part_index * block_width:(part_index + 1) * block_width], preferred_element_type=jnp.float32)
        partial_term = lax.optimization_barrier(partial_term.astype(jnp.bfloat16))
        summed = summed + partial_term.astype(jnp.float32)
    return summed

def assemble(prior_part, new_part, prior_count):
    padded = jnp.concatenate([prior_part, jnp.zeros(new_part.shape, prior_part.dtype)], axis=0)
    return lax.dynamic_update_slice(padded, new_part, (prior_count, jnp.int32(0), jnp.int32(0)))

def reference(tokens, first_gain, first_shift, project_weight, project_bias, output_weight, second_gain, second_shift, expand_weight, contract_weight, prior_cache, prior_len, slot_map, block_table):
    full_width = HEADS * HEAD_DIM
    project_flat = project_weight.reshape(D, 3 * full_width)
    expand_flat = expand_weight.reshape(D, 2 * FF)

    def one_request(operands):
        token_rows, cached, prior_count = operands
        stretch_len = token_rows.shape[0]
        inputs = token_rows.astype(jnp.float32)
        normed = layer_norm(inputs, first_gain, first_shift)
        projected = jnp.dot(normed, project_flat, preferred_element_type=jnp.float32).reshape(stretch_len, 3, full_width) + project_bias
        positions = prior_count + jnp.arange(stretch_len, dtype=jnp.int32)
        queries = rotate(projected[:, 0].reshape(stretch_len, HEADS, HEAD_DIM), positions).astype(jnp.bfloat16)
        new_keys = rotate(projected[:, 1].reshape(stretch_len, HEADS, HEAD_DIM), positions).astype(jnp.bfloat16)
        new_values = projected[:, 2].reshape(stretch_len, HEADS, HEAD_DIM).astype(jnp.bfloat16)
        key_rows = jnp.concatenate([cached[:, 0].reshape(MAX_PRIOR, HEADS, HEAD_DIM), new_keys], axis=0)
        value_rows = jnp.concatenate([cached[:, 1].reshape(MAX_PRIOR, HEADS, HEAD_DIM), new_values], axis=0)
        mixture = attend(queries, key_rows, value_rows, prior_count).reshape(stretch_len, full_width)
        residual = (inputs + summed_parts(mixture, output_weight)).astype(jnp.bfloat16)
        second_normed = layer_norm(residual.astype(jnp.float32), second_gain, second_shift)
        gate_up = jnp.dot(second_normed, expand_flat, preferred_element_type=jnp.float32).reshape(stretch_len, 2, FF)
        hidden = (jax.nn.silu(gate_up[:, 0]) * gate_up[:, 1]).astype(jnp.bfloat16)
        result = (residual.astype(jnp.float32) + summed_parts(hidden, contract_weight)).astype(jnp.bfloat16)
        kept_rows = jnp.arange(MAX_PRIOR, dtype=jnp.int32)[:, None, None] < prior_count
        masked = jnp.where(kept_rows, cached, jnp.zeros((), jnp.bfloat16))
        fresh_cache = jnp.stack([new_keys.reshape(stretch_len, full_width), new_values.reshape(stretch_len, full_width)], axis=1)
        return (result, assemble(masked, fresh_cache, prior_count))
    outputs, caches = lax.map(one_request, (tokens.reshape(REQUESTS, STRETCH, D), prior_cache, prior_len))
    half_width = full_width // 2
    local_half = half_width // N_TP
    groups = REQUESTS // 2
    inverse = jnp.zeros((REQUESTS,), jnp.int32).at[slot_map].set(jnp.arange(REQUESTS, dtype=jnp.int32))
    by_slot = caches[inverse].reshape(REQUESTS, BLOCKS, BLOCK, 2, N_TP, 2, local_half)
    by_slot = by_slot.transpose(0, 5, 1, 2, 3, 4, 6).reshape(groups, 2, 2, BLOCKS, BLOCK, 2, half_width)
    page_items = by_slot.transpose(0, 2, 1, 3, 4, 5, 6).reshape(REQUESTS, 2 * BLOCKS, BLOCK, 2, half_width)
    page_ids = jnp.broadcast_to(block_table.reshape(groups, 1, 2 * BLOCKS), (groups, 2, 2 * BLOCKS)).reshape(REQUESTS, 2 * BLOCKS)
    owners = jnp.broadcast_to(jnp.arange(REQUESTS, dtype=jnp.int32)[:, None], page_ids.shape)
    page_pool = jnp.zeros((REQUESTS, PAGES, BLOCK, 2, half_width), jnp.bfloat16).at[owners, page_ids].set(page_items)
    return (outputs.reshape(TOKENS, D), page_pool)
```

```python
import jax
import jax.numpy as jnp
from jax import lax
from jax.experimental import pallas as pl
from jax.experimental.pallas import tpu as pltpu
from jax.sharding import PartitionSpec as P

HEAD_DIM = 64
ROTARY = 16
BLOCK = 256


EPSILON = 1e-05
ROPE_BASE = 10000.0
MASK_FILL = -1e30


def layer_norm(inputs, gain_row, shift_row):
    center = inputs - jnp.mean(inputs, axis=-1, keepdims=True)
    spread = jnp.mean(center * center, axis=-1, keepdims=True)
    return (center * lax.rsqrt(spread + EPSILON) * gain_row + shift_row).astype(jnp.bfloat16)


def rotate(values, positions):
    half_rot = ROTARY // 2
    frequency = ROPE_BASE ** (-2.0 * jnp.arange(half_rot, dtype=jnp.float32) / ROTARY)
    angles = positions.astype(jnp.float32)[:, None] * frequency[None, :]
    cosine = jnp.cos(angles)[:, None, :]
    sine_part = jnp.sin(angles)[:, None, :]
    first_half = values[..., :half_rot]
    second_half = values[..., half_rot:ROTARY]
    return jnp.concatenate(
        [
            first_half * cosine - second_half * sine_part,
            second_half * cosine + first_half * sine_part,
            values[..., ROTARY:],
        ],
        axis=-1,
    )


def attend(queries, key_rows, value_rows, prior_count):
    query_count = queries.shape[0]
    cache_rows = key_rows.shape[0] - query_count
    scores = jnp.einsum(
        "qhd,khd->hqk", queries, key_rows, preferred_element_type=jnp.float32
    ) * HEAD_DIM ** (-0.5)
    key_index = jnp.arange(key_rows.shape[0], dtype=jnp.int32)[None, :]
    query_index = jnp.arange(query_count, dtype=jnp.int32)[:, None]
    allowed = jnp.where(
        key_index < cache_rows, key_index < prior_count, key_index - cache_rows <= query_index
    )
    scores = jnp.where(allowed[None], scores, MASK_FILL)
    highest = jnp.max(scores, axis=-1, keepdims=True)
    weights = jnp.exp(scores - highest)
    normalized = (weights / jnp.sum(weights, axis=-1, keepdims=True)).astype(jnp.bfloat16)
    mixture = jnp.einsum("hqk,khd->qhd", normalized, value_rows, preferred_element_type=jnp.float32)
    return mixture.astype(jnp.bfloat16)


def regroup(pieces, by_slot):
    count, span_len, _, width = pieces.shape
    half_width = width // 2

    def kernel(by_slot_ref, pieces_ref, out_ref, sems):
        copies = []
        for device in range(count):
            for slot in range(2):
                source = by_slot_ref[2 * (device // 2) + slot]
                columns = pl.ds((device % 2) * half_width, half_width)
                copies.append(
                    pltpu.make_async_copy(
                        pieces_ref.at[source, :, :, columns],
                        out_ref.at[device, slot],
                        sems.at[2 * device + slot],
                    )
                )
                copies[-1].start()
        for copy in copies:
            copy.wait()

    return pl.pallas_call(
        kernel,
        out_shape=jax.ShapeDtypeStruct((count, 2, span_len, 2, half_width), pieces.dtype),
        in_specs=[pl.BlockSpec(memory_space=pltpu.SMEM), pl.BlockSpec(memory_space=pl.ANY)],
        out_specs=pl.BlockSpec(memory_space=pl.ANY),
        scratch_shapes=[pltpu.SemaphoreType.DMA((2 * count,))],
        cost_estimate=pl.CostEstimate(flops=0, bytes_accessed=4 * pieces.size, transcendentals=0),
        name="regroup",
    )(by_slot, pieces)


def place_pages(prior_rows, new_rows, lengths, pages):
    count, _, prior_span, _, width = prior_rows.shape
    new_span = new_rows.shape[2]
    prior_total, new_total = count * prior_span, count * new_span
    blocks = (prior_total + new_total) // BLOCK
    tail = prior_total // BLOCK

    def kernel(lengths_ref, pages_ref, prior_ref, new_ref, zero_ref, pool_ref, rows, *sems):
        prior_sems, new_sems, zero_sems, page_sems = sems
        copies = []
        for slot in range(2):
            for piece in range(count):
                copies.append(
                    pltpu.make_async_copy(
                        prior_ref.at[piece, slot],
                        rows.at[slot, pl.ds(piece * prior_span, prior_span)],
                        prior_sems.at[slot * count + piece],
                    )
                )
                copies[-1].start()
        for copy in copies:
            copy.wait()
        copies = []
        for slot in range(2):
            length = lengths_ref[slot]
            for piece in range(count):
                copies.append(
                    pltpu.make_async_copy(
                        new_ref.at[piece, slot],
                        rows.at[slot, pl.ds(length + piece * new_span, new_span)],
                        new_sems.at[slot * count + piece],
                    )
                )
                copies[-1].start()
            for piece in range(tail):
                copies.append(
                    pltpu.make_async_copy(
                        zero_ref,
                        rows.at[slot, pl.ds(length + new_total + piece * BLOCK, BLOCK)],
                        zero_sems.at[slot * tail + piece],
                    )
                )
                copies[-1].start()
        for copy in copies:
            copy.wait()
        copies = []
        for slot in range(2):
            for block in range(blocks):
                copies.append(
                    pltpu.make_async_copy(
                        rows.at[slot, pl.ds(block * BLOCK, BLOCK)],
                        pool_ref.at[pages_ref[slot * blocks + block]],
                        page_sems.at[slot * blocks + block],
                    )
                )
                copies[-1].start()
        for copy in copies:
            copy.wait()

    return pl.pallas_call(
        kernel,
        out_shape=jax.ShapeDtypeStruct((2 * blocks, BLOCK, 2, width), prior_rows.dtype),
        in_specs=[pl.BlockSpec(memory_space=pltpu.SMEM)] * 2
        + [pl.BlockSpec(memory_space=pl.ANY)] * 3,
        out_specs=pl.BlockSpec(memory_space=pl.ANY),
        scratch_shapes=[
            pltpu.VMEM((2, 2 * prior_total + new_total, 2, width), prior_rows.dtype),
            pltpu.SemaphoreType.DMA((2 * count,)),
            pltpu.SemaphoreType.DMA((2 * count,)),
            pltpu.SemaphoreType.DMA((2 * tail,)),
            pltpu.SemaphoreType.DMA((2 * blocks,)),
        ],
        compiler_params=pltpu.CompilerParams(vmem_limit_bytes=48 * 1024 * 1024),
        cost_estimate=pl.CostEstimate(
            flops=0, bytes_accessed=4 * (prior_rows.size + new_rows.size), transcendentals=0
        ),
        name="place_pages",
    )(lengths, pages, prior_rows, new_rows, jnp.zeros((BLOCK, 2, width), prior_rows.dtype))


NEAR = [(0, 1), (1, 0), (2, 3), (3, 2)]
FAR = [(0, 2), (2, 0), (1, 3), (3, 1)]


def gather_columns(share):
    me = lax.axis_index("tp")
    odd, high = me % 2 == 1, me >= 2
    far = lax.ppermute(share, "tp", FAR)
    near = lax.ppermute(share, "tp", NEAR)
    far_near = lax.ppermute(far, "tp", NEAR)
    own_first, own_second = jnp.where(odd, near, share), jnp.where(odd, share, near)
    far_first, far_second = jnp.where(odd, far_near, far), jnp.where(odd, far, far_near)
    return jnp.concatenate(
        [
            jnp.where(high, far_first, own_first),
            jnp.where(high, far_second, own_second),
            jnp.where(high, own_first, far_first),
            jnp.where(high, own_second, far_second),
        ],
        axis=1,
    )


def scatter_sum(partial):
    me = lax.axis_index("tp")
    odd, high = me % 2 == 1, me >= 2
    width = partial.shape[1] // 4
    blocks = [partial[:, at * width : (at + 1) * width] for at in range(4)]

    def near_sum(even_block, odd_block):
        received = lax.ppermute(jnp.where(odd, even_block, odd_block), "tp", NEAR)
        return jnp.where(odd, odd_block, even_block).astype(jnp.float32) + received.astype(
            jnp.float32
        )

    low_half = near_sum(blocks[0], blocks[1])
    high_half = near_sum(blocks[2], blocks[3])
    leaving = jnp.where(high, low_half, high_half).astype(jnp.bfloat16)
    received = lax.ppermute(leaving, "tp", FAR)
    return jnp.where(high, high_half, low_half) + received.astype(jnp.float32)


def local(
    tokens,
    first_gain,
    first_shift,
    project_weight,
    project_bias,
    output_weight,
    second_gain,
    second_shift,
    expand_weight,
    contract_weight,
    prior_cache,
    prior_len,
    slot_map,
    block_table,
):
    request = lax.axis_index("req")
    prior_count = prior_len[request]
    stretch_len = tokens.shape[0]
    local_width = project_weight.shape[2]
    local_heads = local_width // HEAD_DIM
    local_hidden = expand_weight.shape[2]
    cached = prior_cache[0]
    req_count = slot_map.shape[0]
    cache_len = cached.shape[0]
    by_slot = jnp.sum(
        jnp.where(
            slot_map[None, :] == jnp.arange(req_count, dtype=jnp.int32)[:, None],
            jnp.arange(req_count, dtype=jnp.int32)[None, :],
            0,
        ),
        axis=1,
    )
    prior_pieces = lax.all_to_all(
        cached.reshape(req_count, cache_len // req_count, 2, local_width),
        "req",
        split_axis=0,
        concat_axis=0,
        tiled=True,
    )
    prior_received = lax.all_to_all(
        regroup(prior_pieces, by_slot), "req", split_axis=0, concat_axis=0, tiled=True
    )
    token_rows = gather_columns(tokens)
    inputs = token_rows.astype(jnp.float32)
    normed = layer_norm(inputs, first_gain, first_shift)
    projected = (
        jnp.dot(
            normed,
            project_weight.reshape(project_weight.shape[0], 3 * local_width),
            preferred_element_type=jnp.float32,
        ).reshape(stretch_len, 3, local_width)
        + project_bias
    )
    positions = prior_count + jnp.arange(stretch_len, dtype=jnp.int32)
    queries = rotate(projected[:, 0].reshape(stretch_len, local_heads, HEAD_DIM), positions).astype(
        jnp.bfloat16
    )
    new_keys = rotate(
        projected[:, 1].reshape(stretch_len, local_heads, HEAD_DIM), positions
    ).astype(jnp.bfloat16)
    new_values = projected[:, 2].reshape(stretch_len, local_heads, HEAD_DIM).astype(jnp.bfloat16)
    key_rows = jnp.concatenate(
        [cached[:, 0].reshape(cache_len, local_heads, HEAD_DIM), new_keys], axis=0
    )
    value_rows = jnp.concatenate(
        [cached[:, 1].reshape(cache_len, local_heads, HEAD_DIM), new_values], axis=0
    )
    mixture = attend(queries, key_rows, value_rows, prior_count).reshape(stretch_len, local_width)
    partial_value = jnp.dot(mixture, output_weight, preferred_element_type=jnp.float32)
    mixer_share = scatter_sum(partial_value.astype(jnp.bfloat16))
    residual_share = (tokens.astype(jnp.float32) + mixer_share).astype(jnp.bfloat16)
    residual = gather_columns(residual_share)
    second_normed = layer_norm(residual.astype(jnp.float32), second_gain, second_shift)
    gate_up = jnp.dot(
        second_normed,
        expand_weight.reshape(expand_weight.shape[0], 2 * local_hidden),
        preferred_element_type=jnp.float32,
    ).reshape(stretch_len, 2, local_hidden)
    hidden = (jax.nn.silu(gate_up[:, 0]) * gate_up[:, 1]).astype(jnp.bfloat16)
    down_share = scatter_sum(
        jnp.dot(hidden, contract_weight, preferred_element_type=jnp.float32).astype(jnp.bfloat16)
    )
    result = (residual_share.astype(jnp.float32) + down_share).astype(jnp.bfloat16)
    fresh_cache = jnp.stack(
        [new_keys.reshape(stretch_len, local_width), new_values.reshape(stretch_len, local_width)],
        axis=1,
    )
    new_pieces = lax.all_to_all(
        fresh_cache.reshape(req_count, stretch_len // req_count, 2, local_width),
        "req",
        split_axis=0,
        concat_axis=0,
        tiled=True,
    )
    new_received = lax.all_to_all(
        regroup(new_pieces, by_slot), "req", split_axis=0, concat_axis=0, tiled=True
    )
    group_index = request // 2
    slots = lax.dynamic_slice_in_dim(by_slot, 2 * group_index, 2, 0)
    lengths = jnp.take(prior_len, slots)
    pages = lax.dynamic_slice_in_dim(block_table, 2 * group_index, 2, 0).reshape(-1)
    page_pool = place_pages(prior_received, new_received, lengths, pages)[None]
    return (result, page_pool)


def solution(mesh):
    return jax.shard_map(
        local,
        mesh=mesh,
        in_specs=(
            P("req", "tp"),
            P(),
            P(),
            P(None, None, "tp"),
            P(None, "tp"),
            P("tp", None),
            P(),
            P(),
            P(None, None, "tp"),
            P("tp", None),
            P("req", None, None, "tp"),
            P(),
            P(),
            P(),
        ),
        out_specs=(P("req", "tp"), P("req", None, None, None, "tp")),
        check_vma=False,
    )
```

```python
import jax
import jax.numpy as jnp
from jax import lax
from jax.experimental import pallas as pl
from jax.experimental.pallas import tpu as pltpu
from jax.sharding import PartitionSpec as P

HEAD_DIM = 64
ROTARY = 16
BLOCK = 256


EPSILON = 1e-05
ROPE_BASE = 10000.0
MASK_FILL = -1e30


def layer_norm(inputs, gain_row, shift_row):
    center = inputs - jnp.mean(inputs, axis=-1, keepdims=True)
    spread = jnp.mean(center * center, axis=-1, keepdims=True)
    return (center * lax.rsqrt(spread + EPSILON) * gain_row + shift_row).astype(jnp.bfloat16)


def turns(positions, width):
    half_rot = ROTARY // 2
    feature = jnp.arange(2 * HEAD_DIM, dtype=jnp.int32) % HEAD_DIM
    rate = ROPE_BASE ** (-2.0 * (feature % half_rot).astype(jnp.float32) / ROTARY)
    frequency = jnp.where(feature < ROTARY, rate, 0.0)
    angles = positions.astype(jnp.float32)[:, None] * frequency[None, :]
    cosine, sine_part = jnp.cos(angles), jnp.sin(angles)
    first = jnp.where((feature < half_rot)[None, :], -sine_part, 0.0)
    second = jnp.where((feature >= half_rot)[None, :], sine_part, 0.0)
    repeats = width // (2 * HEAD_DIM)
    return [jnp.concatenate([part] * repeats, axis=1) for part in (cosine, first, second)]


def rotate(values, cosine, first, second):
    half_rot = ROTARY // 2
    return (
        values * cosine
        + jnp.roll(values, -half_rot, axis=1) * first
        + jnp.roll(values, half_rot, axis=1) * second
    )


def attend(queries, key_rows, value_rows, prior_count):
    query_count = queries.shape[0]
    cache_rows = key_rows.shape[0] - query_count
    scores = jnp.einsum(
        "qhd,khd->hqk", queries, key_rows, preferred_element_type=jnp.float32
    ) * HEAD_DIM ** (-0.5)
    key_index = jnp.arange(key_rows.shape[0], dtype=jnp.int32)[None, :]
    query_index = jnp.arange(query_count, dtype=jnp.int32)[:, None]
    allowed = jnp.where(
        key_index < cache_rows, key_index < prior_count, key_index - cache_rows <= query_index
    )
    scores = jnp.where(allowed[None], scores, MASK_FILL)
    highest = jnp.max(scores, axis=-1, keepdims=True)
    weights = jnp.exp(scores - highest)
    normalized = (weights / jnp.sum(weights, axis=-1, keepdims=True)).astype(jnp.bfloat16)
    mixture = jnp.einsum("hqk,khd->qhd", normalized, value_rows, preferred_element_type=jnp.float32)
    return mixture.astype(jnp.bfloat16)


def regroup(pieces, by_slot):
    count, span_len, _, width = pieces.shape
    half_width = width // 2

    def kernel(by_slot_ref, pieces_ref, out_ref, held, in_sems, out_sems):
        fetches, stores = [], []
        for device in range(count):
            for slot in range(2):
                source = by_slot_ref[2 * (device // 2) + slot]
                columns = pl.ds((device % 2) * half_width, half_width)
                fetches.append(
                    pltpu.make_async_copy(
                        pieces_ref.at[source, :, :, columns],
                        held.at[device, slot],
                        in_sems.at[2 * device + slot],
                    )
                )
                stores.append(
                    pltpu.make_async_copy(
                        held.at[device, slot],
                        out_ref.at[device, slot],
                        out_sems.at[2 * device + slot],
                    )
                )
                fetches[-1].start()
        for fetch, store in zip(fetches, stores):
            fetch.wait()
            store.start()
        for store in stores:
            store.wait()

    return pl.pallas_call(
        kernel,
        out_shape=jax.ShapeDtypeStruct((count, 2, span_len, 2, half_width), pieces.dtype),
        in_specs=[pl.BlockSpec(memory_space=pltpu.SMEM), pl.BlockSpec(memory_space=pl.ANY)],
        out_specs=pl.BlockSpec(memory_space=pl.ANY),
        scratch_shapes=[
            pltpu.VMEM((count, 2, span_len, 2, half_width), pieces.dtype),
            pltpu.SemaphoreType.DMA((2 * count,)),
            pltpu.SemaphoreType.DMA((2 * count,)),
        ],
        compiler_params=pltpu.CompilerParams(vmem_limit_bytes=24 * 1024 * 1024),
        cost_estimate=pl.CostEstimate(flops=0, bytes_accessed=4 * pieces.size, transcendentals=0),
        name="regroup",
    )(by_slot, pieces)


def place_pages(prior_rows, new_rows, lengths, pages):
    count, _, prior_span, _, width = prior_rows.shape
    new_span = new_rows.shape[2]
    prior_total, new_total = count * prior_span, count * new_span
    blocks = (prior_total + new_total) // BLOCK
    tail = prior_total // BLOCK

    def kernel(lengths_ref, pages_ref, prior_ref, new_ref, zero_ref, pool_ref, rows, *sems):
        prior_sems, new_sems, zero_sems, page_sems = sems
        copies = []
        for slot in range(2):
            for piece in range(count):
                copies.append(
                    pltpu.make_async_copy(
                        prior_ref.at[piece, slot],
                        rows.at[slot, pl.ds(piece * prior_span, prior_span)],
                        prior_sems.at[slot * count + piece],
                    )
                )
                copies[-1].start()
        for copy in copies:
            copy.wait()
        copies = []
        for slot in range(2):
            length = lengths_ref[slot]
            for piece in range(count):
                copies.append(
                    pltpu.make_async_copy(
                        new_ref.at[piece, slot],
                        rows.at[slot, pl.ds(length + piece * new_span, new_span)],
                        new_sems.at[slot * count + piece],
                    )
                )
                copies[-1].start()
            for piece in range(tail):
                copies.append(
                    pltpu.make_async_copy(
                        zero_ref,
                        rows.at[slot, pl.ds(length + new_total + piece * BLOCK, BLOCK)],
                        zero_sems.at[slot * tail + piece],
                    )
                )
                copies[-1].start()
        for copy in copies:
            copy.wait()
        copies = []
        for slot in range(2):
            for block in range(blocks):
                copies.append(
                    pltpu.make_async_copy(
                        rows.at[slot, pl.ds(block * BLOCK, BLOCK)],
                        pool_ref.at[pages_ref[slot * blocks + block]],
                        page_sems.at[slot * blocks + block],
                    )
                )
                copies[-1].start()
        for copy in copies:
            copy.wait()

    return pl.pallas_call(
        kernel,
        out_shape=jax.ShapeDtypeStruct((2 * blocks, BLOCK, 2, width), prior_rows.dtype),
        in_specs=[pl.BlockSpec(memory_space=pltpu.SMEM)] * 2
        + [pl.BlockSpec(memory_space=pl.ANY)] * 3,
        out_specs=pl.BlockSpec(memory_space=pl.ANY),
        scratch_shapes=[
            pltpu.VMEM((2, 2 * prior_total + new_total, 2, width), prior_rows.dtype),
            pltpu.SemaphoreType.DMA((2 * count,)),
            pltpu.SemaphoreType.DMA((2 * count,)),
            pltpu.SemaphoreType.DMA((2 * tail,)),
            pltpu.SemaphoreType.DMA((2 * blocks,)),
        ],
        compiler_params=pltpu.CompilerParams(vmem_limit_bytes=48 * 1024 * 1024),
        cost_estimate=pl.CostEstimate(
            flops=0, bytes_accessed=4 * (prior_rows.size + new_rows.size), transcendentals=0
        ),
        name="place_pages",
    )(lengths, pages, prior_rows, new_rows, jnp.zeros((BLOCK, 2, width), prior_rows.dtype))


NEAR = [(0, 1), (1, 0), (2, 3), (3, 2)]
FAR = [(0, 2), (2, 0), (1, 3), (3, 1)]


def gather_columns(share):
    me = lax.axis_index("tp")
    odd, high = me % 2 == 1, me >= 2
    far = lax.ppermute(share, "tp", FAR)
    near = lax.ppermute(share, "tp", NEAR)
    far_near = lax.ppermute(far, "tp", NEAR)
    own_first, own_second = jnp.where(odd, near, share), jnp.where(odd, share, near)
    far_first, far_second = jnp.where(odd, far_near, far), jnp.where(odd, far, far_near)
    return jnp.concatenate(
        [
            jnp.where(high, far_first, own_first),
            jnp.where(high, far_second, own_second),
            jnp.where(high, own_first, far_first),
            jnp.where(high, own_second, far_second),
        ],
        axis=1,
    )


def scatter_sum(partial):
    me = lax.axis_index("tp")
    odd, high = me % 2 == 1, me >= 2
    width = partial.shape[1] // 4
    blocks = [partial[:, at * width : (at + 1) * width] for at in range(4)]

    def near_sum(even_block, odd_block):
        received = lax.ppermute(jnp.where(odd, even_block, odd_block), "tp", NEAR)
        return jnp.where(odd, odd_block, even_block).astype(jnp.float32) + received.astype(
            jnp.float32
        )

    low_half = near_sum(blocks[0], blocks[1])
    high_half = near_sum(blocks[2], blocks[3])
    leaving = jnp.where(high, low_half, high_half).astype(jnp.bfloat16)
    received = lax.ppermute(leaving, "tp", FAR)
    return jnp.where(high, high_half, low_half) + received.astype(jnp.float32)


def local(
    tokens,
    first_gain,
    first_shift,
    project_weight,
    project_bias,
    output_weight,
    second_gain,
    second_shift,
    expand_weight,
    contract_weight,
    prior_cache,
    prior_len,
    slot_map,
    block_table,
):
    request = lax.axis_index("req")
    prior_count = prior_len[request]
    stretch_len = tokens.shape[0]
    local_width = project_weight.shape[2]
    local_heads = local_width // HEAD_DIM
    local_hidden = expand_weight.shape[2]
    cached = prior_cache[0]
    req_count = slot_map.shape[0]
    cache_len = cached.shape[0]
    by_slot = jnp.sum(
        jnp.where(
            slot_map[None, :] == jnp.arange(req_count, dtype=jnp.int32)[:, None],
            jnp.arange(req_count, dtype=jnp.int32)[None, :],
            0,
        ),
        axis=1,
    )
    prior_pieces = lax.all_to_all(
        cached.reshape(req_count, cache_len // req_count, 2, local_width),
        "req",
        split_axis=0,
        concat_axis=0,
        tiled=True,
    )
    token_rows = gather_columns(tokens)
    inputs = token_rows.astype(jnp.float32)
    normed = layer_norm(inputs, first_gain, first_shift)
    projected = [
        jnp.dot(normed, project_weight[:, part], preferred_element_type=jnp.float32)
        + project_bias[part]
        for part in range(3)
    ]
    positions = prior_count + jnp.arange(stretch_len, dtype=jnp.int32)
    angle_parts = turns(positions, local_width)
    flat_queries = rotate(projected[0], *angle_parts).astype(jnp.bfloat16)
    flat_keys = rotate(projected[1], *angle_parts).astype(jnp.bfloat16)
    flat_values = projected[2].astype(jnp.bfloat16)
    queries = flat_queries.reshape(stretch_len, local_heads, HEAD_DIM)
    new_keys = flat_keys.reshape(stretch_len, local_heads, HEAD_DIM)
    new_values = flat_values.reshape(stretch_len, local_heads, HEAD_DIM)
    key_rows = jnp.concatenate(
        [cached[:, 0].reshape(cache_len, local_heads, HEAD_DIM), new_keys], axis=0
    )
    value_rows = jnp.concatenate(
        [cached[:, 1].reshape(cache_len, local_heads, HEAD_DIM), new_values], axis=0
    )
    mixture = attend(queries, key_rows, value_rows, prior_count).reshape(stretch_len, local_width)
    partial_value = jnp.dot(mixture, output_weight, preferred_element_type=jnp.float32)
    mixer_share = scatter_sum(partial_value.astype(jnp.bfloat16))
    residual_share = (tokens.astype(jnp.float32) + mixer_share).astype(jnp.bfloat16)
    residual = gather_columns(residual_share)
    second_normed = layer_norm(residual.astype(jnp.float32), second_gain, second_shift)
    gate_up = jnp.dot(
        second_normed,
        expand_weight.reshape(expand_weight.shape[0], 2 * local_hidden),
        preferred_element_type=jnp.float32,
    ).reshape(stretch_len, 2, local_hidden)
    hidden = (jax.nn.silu(gate_up[:, 0]) * gate_up[:, 1]).astype(jnp.bfloat16)
    down_share = scatter_sum(
        jnp.dot(hidden, contract_weight, preferred_element_type=jnp.float32).astype(jnp.bfloat16)
    )
    result = (residual_share.astype(jnp.float32) + down_share).astype(jnp.bfloat16)
    fresh_cache = jnp.stack([flat_keys, flat_values], axis=1)
    fresh_cache, prior_pieces = lax.optimization_barrier((fresh_cache, prior_pieces))
    new_pieces = lax.all_to_all(
        fresh_cache.reshape(req_count, stretch_len // req_count, 2, local_width),
        "req",
        split_axis=0,
        concat_axis=0,
        tiled=True,
    )
    prior_ordered, new_pieces = lax.optimization_barrier(
        (regroup(prior_pieces, by_slot), new_pieces)
    )
    prior_received = lax.all_to_all(
        prior_ordered, "req", split_axis=0, concat_axis=0, tiled=True
    )
    new_ordered, prior_received = lax.optimization_barrier(
        (regroup(new_pieces, by_slot), prior_received)
    )
    new_received = lax.all_to_all(new_ordered, "req", split_axis=0, concat_axis=0, tiled=True)
    group_index = request // 2
    slots = lax.dynamic_slice_in_dim(by_slot, 2 * group_index, 2, 0)
    lengths = jnp.take(prior_len, slots)
    pages = lax.dynamic_slice_in_dim(block_table, 2 * group_index, 2, 0).reshape(-1)
    page_pool = place_pages(prior_received, new_received, lengths, pages)[None]
    return (result, page_pool)


def solution(mesh):
    return jax.shard_map(
        local,
        mesh=mesh,
        in_specs=(
            P("req", "tp"),
            P(),
            P(),
            P(None, None, "tp"),
            P(None, "tp"),
            P("tp", None),
            P(),
            P(),
            P(None, None, "tp"),
            P("tp", None),
            P("req", None, None, "tp"),
            P(),
            P(),
            P(),
        ),
        out_specs=(P("req", "tp"), P("req", None, None, None, "tp")),
        check_vma=False,
    )
```

```python
import jax
import jax.numpy as jnp
from jax import lax
from jax.experimental import pallas as pl
from jax.experimental.pallas import tpu as pltpu
from jax.sharding import PartitionSpec as P

HEAD_DIM = 64
ROTARY = 16
BLOCK = 256


EPSILON = 1e-05
ROPE_BASE = 10000.0
MASK_FILL = -1e30


def layer_norm(inputs, gain_row, shift_row):
    center = inputs - jnp.mean(inputs, axis=-1, keepdims=True)
    spread = jnp.mean(center * center, axis=-1, keepdims=True)
    return (center * lax.rsqrt(spread + EPSILON) * gain_row + shift_row).astype(jnp.bfloat16)


def turns(positions, width):
    half_rot = ROTARY // 2
    feature = jnp.arange(2 * HEAD_DIM, dtype=jnp.int32) % HEAD_DIM
    rate = ROPE_BASE ** (-2.0 * (feature % half_rot).astype(jnp.float32) / ROTARY)
    frequency = jnp.where(feature < ROTARY, rate, 0.0)
    angles = positions.astype(jnp.float32)[:, None] * frequency[None, :]
    cosine, sine_part = jnp.cos(angles), jnp.sin(angles)
    first = jnp.where((feature < half_rot)[None, :], -sine_part, 0.0)
    second = jnp.where((feature >= half_rot)[None, :], sine_part, 0.0)
    repeats = width // (2 * HEAD_DIM)
    return [jnp.concatenate([part] * repeats, axis=1) for part in (cosine, first, second)]


def rotate(values, cosine, first, second):
    half_rot = ROTARY // 2
    return (
        values * cosine
        + jnp.roll(values, -half_rot, axis=1) * first
        + jnp.roll(values, half_rot, axis=1) * second
    )


def attend(queries, key_rows, value_rows, prior_count):
    query_count = queries.shape[0]
    cache_rows = key_rows.shape[0] - query_count
    scores = jnp.einsum(
        "qhd,khd->hqk", queries, key_rows, preferred_element_type=jnp.float32
    ) * HEAD_DIM ** (-0.5)
    key_index = jnp.arange(key_rows.shape[0], dtype=jnp.int32)[None, :]
    query_index = jnp.arange(query_count, dtype=jnp.int32)[:, None]
    allowed = jnp.where(
        key_index < cache_rows, key_index < prior_count, key_index - cache_rows <= query_index
    )
    scores = jnp.where(allowed[None], scores, MASK_FILL)
    highest = jnp.max(scores, axis=-1, keepdims=True)
    weights = jnp.exp(scores - highest)
    normalized = (weights / jnp.sum(weights, axis=-1, keepdims=True)).astype(jnp.bfloat16)
    mixture = jnp.einsum("hqk,khd->qhd", normalized, value_rows, preferred_element_type=jnp.float32)
    return mixture.astype(jnp.bfloat16)


def regroup(pieces, by_slot):
    count, span_len, _, width = pieces.shape
    half_width = width // 2

    def kernel(by_slot_ref, pieces_ref, out_ref, held, in_sems, out_sems):
        fetches, stores = [], []
        for device in range(count):
            for slot in range(2):
                source = by_slot_ref[2 * (device // 2) + slot]
                columns = pl.ds((device % 2) * half_width, half_width)
                fetches.append(
                    pltpu.make_async_copy(
                        pieces_ref.at[source, :, :, columns],
                        held.at[device, slot],
                        in_sems.at[2 * device + slot],
                    )
                )
                stores.append(
                    pltpu.make_async_copy(
                        held.at[device, slot],
                        out_ref.at[device, slot],
                        out_sems.at[2 * device + slot],
                    )
                )
                fetches[-1].start()
        for fetch, store in zip(fetches, stores):
            fetch.wait()
            store.start()
        for store in stores:
            store.wait()

    return pl.pallas_call(
        kernel,
        out_shape=jax.ShapeDtypeStruct((count, 2, span_len, 2, half_width), pieces.dtype),
        in_specs=[pl.BlockSpec(memory_space=pltpu.SMEM), pl.BlockSpec(memory_space=pl.ANY)],
        out_specs=pl.BlockSpec(memory_space=pl.ANY),
        scratch_shapes=[
            pltpu.VMEM((count, 2, span_len, 2, half_width), pieces.dtype),
            pltpu.SemaphoreType.DMA((2 * count,)),
            pltpu.SemaphoreType.DMA((2 * count,)),
        ],
        compiler_params=pltpu.CompilerParams(vmem_limit_bytes=24 * 1024 * 1024),
        cost_estimate=pl.CostEstimate(flops=0, bytes_accessed=4 * pieces.size, transcendentals=0),
        name="regroup",
    )(by_slot, pieces)


def place_pages(prior_rows, new_rows, lengths, pages):
    count, _, prior_span, _, width = prior_rows.shape
    new_span = new_rows.shape[2]
    prior_total, new_total = count * prior_span, count * new_span
    blocks = (prior_total + new_total) // BLOCK
    tail = prior_total // BLOCK

    def kernel(lengths_ref, pages_ref, prior_ref, new_ref, zero_ref, pool_ref, rows, *sems):
        prior_sems, new_sems, zero_sems, page_sems = sems
        copies = []
        for slot in range(2):
            for piece in range(count):
                copies.append(
                    pltpu.make_async_copy(
                        prior_ref.at[piece, slot],
                        rows.at[slot, pl.ds(piece * prior_span, prior_span)],
                        prior_sems.at[slot * count + piece],
                    )
                )
                copies[-1].start()
        for copy in copies:
            copy.wait()
        copies = []
        for slot in range(2):
            length = lengths_ref[slot]
            for piece in range(count):
                copies.append(
                    pltpu.make_async_copy(
                        new_ref.at[piece, slot],
                        rows.at[slot, pl.ds(length + piece * new_span, new_span)],
                        new_sems.at[slot * count + piece],
                    )
                )
                copies[-1].start()
            for piece in range(tail):
                copies.append(
                    pltpu.make_async_copy(
                        zero_ref,
                        rows.at[slot, pl.ds(length + new_total + piece * BLOCK, BLOCK)],
                        zero_sems.at[slot * tail + piece],
                    )
                )
                copies[-1].start()
        for copy in copies:
            copy.wait()
        copies = []
        for slot in range(2):
            for block in range(blocks):
                copies.append(
                    pltpu.make_async_copy(
                        rows.at[slot, pl.ds(block * BLOCK, BLOCK)],
                        pool_ref.at[pages_ref[slot * blocks + block]],
                        page_sems.at[slot * blocks + block],
                    )
                )
                copies[-1].start()
        for copy in copies:
            copy.wait()

    return pl.pallas_call(
        kernel,
        out_shape=jax.ShapeDtypeStruct((2 * blocks, BLOCK, 2, width), prior_rows.dtype),
        in_specs=[pl.BlockSpec(memory_space=pltpu.SMEM)] * 2
        + [pl.BlockSpec(memory_space=pl.ANY)] * 3,
        out_specs=pl.BlockSpec(memory_space=pl.ANY),
        scratch_shapes=[
            pltpu.VMEM((2, 2 * prior_total + new_total, 2, width), prior_rows.dtype),
            pltpu.SemaphoreType.DMA((2 * count,)),
            pltpu.SemaphoreType.DMA((2 * count,)),
            pltpu.SemaphoreType.DMA((2 * tail,)),
            pltpu.SemaphoreType.DMA((2 * blocks,)),
        ],
        compiler_params=pltpu.CompilerParams(vmem_limit_bytes=48 * 1024 * 1024),
        cost_estimate=pl.CostEstimate(
            flops=0, bytes_accessed=4 * (prior_rows.size + new_rows.size), transcendentals=0
        ),
        name="place_pages",
    )(lengths, pages, prior_rows, new_rows, jnp.zeros((BLOCK, 2, width), prior_rows.dtype))


NEAR = [(0, 1), (1, 0), (2, 3), (3, 2)]
FAR = [(0, 2), (2, 0), (1, 3), (3, 1)]


def gather_columns(share):
    me = lax.axis_index("tp")
    odd, high = me % 2 == 1, me >= 2
    far = lax.ppermute(share, "tp", FAR)
    near = lax.ppermute(share, "tp", NEAR)
    far_near = lax.ppermute(far, "tp", NEAR)
    own_first, own_second = jnp.where(odd, near, share), jnp.where(odd, share, near)
    far_first, far_second = jnp.where(odd, far_near, far), jnp.where(odd, far, far_near)
    return jnp.concatenate(
        [
            jnp.where(high, far_first, own_first),
            jnp.where(high, far_second, own_second),
            jnp.where(high, own_first, far_first),
            jnp.where(high, own_second, far_second),
        ],
        axis=1,
    )


def scatter_sum(partial, earlier):
    me = lax.axis_index("tp")
    odd, high = me % 2 == 1, me >= 2
    width = partial.shape[1] // 4
    blocks = [partial[:, at * width : (at + 1) * width] for at in range(4)]

    def near_sum(even_block, odd_block):
        received = lax.ppermute(jnp.where(odd, even_block, odd_block), "tp", NEAR)
        return jnp.where(odd, odd_block, even_block).astype(jnp.float32) + received.astype(
            jnp.float32
        )

    low_half = near_sum(blocks[0], blocks[1])
    high_half = near_sum(blocks[2], blocks[3])
    leaving = jnp.where(high, low_half, high_half).astype(jnp.bfloat16)
    leaving, earlier = lax.optimization_barrier((leaving, earlier))
    received = lax.ppermute(leaving, "tp", FAR)
    return jnp.where(high, high_half, low_half) + received.astype(jnp.float32), earlier


def local(
    tokens,
    first_gain,
    first_shift,
    project_weight,
    project_bias,
    output_weight,
    second_gain,
    second_shift,
    expand_weight,
    contract_weight,
    prior_cache,
    prior_len,
    slot_map,
    block_table,
):
    request = lax.axis_index("req")
    prior_count = prior_len[request]
    stretch_len = tokens.shape[0]
    local_width = project_weight.shape[2]
    local_heads = local_width // HEAD_DIM
    local_hidden = expand_weight.shape[2]
    cached = prior_cache[0]
    req_count = slot_map.shape[0]
    cache_len = cached.shape[0]
    by_slot = jnp.sum(
        jnp.where(
            slot_map[None, :] == jnp.arange(req_count, dtype=jnp.int32)[:, None],
            jnp.arange(req_count, dtype=jnp.int32)[None, :],
            0,
        ),
        axis=1,
    )
    prior_pieces = lax.all_to_all(
        cached.reshape(req_count, cache_len // req_count, 2, local_width),
        "req",
        split_axis=0,
        concat_axis=0,
        tiled=True,
    )
    token_rows = gather_columns(tokens)
    inputs = token_rows.astype(jnp.float32)
    normed = layer_norm(inputs, first_gain, first_shift)
    projected = [
        jnp.dot(normed, project_weight[:, part], preferred_element_type=jnp.float32)
        + project_bias[part]
        for part in range(3)
    ]
    positions = prior_count + jnp.arange(stretch_len, dtype=jnp.int32)
    angle_parts = turns(positions, local_width)
    flat_queries = rotate(projected[0], *angle_parts).astype(jnp.bfloat16)
    flat_keys = rotate(projected[1], *angle_parts).astype(jnp.bfloat16)
    flat_values = projected[2].astype(jnp.bfloat16)
    queries = flat_queries.reshape(stretch_len, local_heads, HEAD_DIM)
    new_keys = flat_keys.reshape(stretch_len, local_heads, HEAD_DIM)
    new_values = flat_values.reshape(stretch_len, local_heads, HEAD_DIM)
    fresh_cache = jnp.stack([flat_keys, flat_values], axis=1)
    fresh_cache, prior_pieces = lax.optimization_barrier((fresh_cache, prior_pieces))
    new_pieces = lax.all_to_all(
        fresh_cache.reshape(req_count, stretch_len // req_count, 2, local_width),
        "req",
        split_axis=0,
        concat_axis=0,
        tiled=True,
    )
    key_rows = jnp.concatenate(
        [cached[:, 0].reshape(cache_len, local_heads, HEAD_DIM), new_keys], axis=0
    )
    value_rows = jnp.concatenate(
        [cached[:, 1].reshape(cache_len, local_heads, HEAD_DIM), new_values], axis=0
    )
    mixture = attend(queries, key_rows, value_rows, prior_count).reshape(stretch_len, local_width)
    partial_value = jnp.dot(mixture, output_weight, preferred_element_type=jnp.float32)
    mixer_share, new_pieces = scatter_sum(partial_value.astype(jnp.bfloat16), new_pieces)
    prior_ordered, new_pieces = lax.optimization_barrier(
        (regroup(prior_pieces, by_slot), new_pieces)
    )
    prior_received = lax.all_to_all(
        prior_ordered, "req", split_axis=0, concat_axis=0, tiled=True
    )
    residual_share = (tokens.astype(jnp.float32) + mixer_share).astype(jnp.bfloat16)
    residual = gather_columns(residual_share)
    second_normed = layer_norm(residual.astype(jnp.float32), second_gain, second_shift)
    second_normed, prior_received = lax.optimization_barrier((second_normed, prior_received))
    gate_up = jnp.dot(
        second_normed,
        expand_weight.reshape(expand_weight.shape[0], 2 * local_hidden),
        preferred_element_type=jnp.float32,
    ).reshape(stretch_len, 2, local_hidden)
    hidden = (jax.nn.silu(gate_up[:, 0]) * gate_up[:, 1]).astype(jnp.bfloat16)
    new_ordered, prior_received = lax.optimization_barrier(
        (regroup(new_pieces, by_slot), prior_received)
    )
    new_received = lax.all_to_all(new_ordered, "req", split_axis=0, concat_axis=0, tiled=True)
    down_share, prior_received = scatter_sum(
        jnp.dot(hidden, contract_weight, preferred_element_type=jnp.float32).astype(jnp.bfloat16),
        prior_received,
    )
    result = (residual_share.astype(jnp.float32) + down_share).astype(jnp.bfloat16)
    group_index = request // 2
    slots = lax.dynamic_slice_in_dim(by_slot, 2 * group_index, 2, 0)
    lengths = jnp.take(prior_len, slots)
    pages = lax.dynamic_slice_in_dim(block_table, 2 * group_index, 2, 0).reshape(-1)
    page_pool = place_pages(prior_received, new_received, lengths, pages)[None]
    return (result, page_pool)


def solution(mesh):
    return jax.shard_map(
        local,
        mesh=mesh,
        in_specs=(
            P("req", "tp"),
            P(),
            P(),
            P(None, None, "tp"),
            P(None, "tp"),
            P("tp", None),
            P(),
            P(),
            P(None, None, "tp"),
            P("tp", None),
            P("req", None, None, "tp"),
            P(),
            P(),
            P(),
        ),
        out_specs=(P("req", "tp"), P("req", None, None, None, "tp")),
        check_vma=False,
    )
```
